32 devices in a mesh: row: 4 (over y, x), col: 8 (over z, core).
Axes of the slice: x: 2, y: 2, z: 4, core: 2. Of those that a mesh axis runs over, the one named last changes fastest.
Arguments:
- rhs: float32 [4, 4, 8, 128, 256], P(None, 'row', 'col'), may hold values from -6 to 6
- diag_inverse: float32 [4, 4, 8, 128, 128], P(None, 'row', 'col'), as said below
- update_blocks: float32 [3, 4, 8, 48, 128, 128], P(None, 'row', 'col'), may hold values from -0.15625 to 0.15625
- source_slot: int32 [3, 4, 8, 48], P(None, 'row', 'col'), may hold values from 0 to 3
- target_slot: int32 [3, 4, 8, 48], P(None, 'row', 'col'), may hold values from 0 to 7
- block_count: int32 [3, 4, 8], P(None, 'row', 'col'), may hold values from 1 to 48, as said below
Outputs:
- forward_solution: float32 [4, 4, 8, 128, 256], P(None, 'row', 'col')
- solution: float32 [4, 4, 8, 128, 256], P(None, 'row', 'col')
The draws below stay inside these ranges and needn't reach their ends.
Inputs may be any that keep to these rules, and one draw needn't show every extreme that they name: Each diag_inverse block is lower triangular with diagonal entries between 0.5 and 1.6. `block_count`: at every level some device uses all 48 slots.
All inputs are finite; a program needn't handle non-finite values.
Results may differ from the reference program's by a relative error of at most 0.0003.
Values sent between devices are 32-bit elements; how exact they have to be, the bound alone decides.
A program may use at most 128 MiB of HBM per device.

```python
import math
import jax
import jax.numpy as jnp
from jax import lax

S = 128
NRHS = 256
LEVELS = 4
NB = 48
ROWS_SN = 4
COLS_SN = 8


def draw_diag_inverse(key, part):
    key_diag, second = jax.random.split(key)
    layout = (LEVELS, ROWS_SN, COLS_SN, S)
    diagonal = jnp.exp(jax.random.uniform(key_diag, layout, jnp.float32, math.log(0.5), math.log(1.6)))
    lower_part = jnp.clip(jax.random.normal(second, layout + (S,), jnp.float32), -4.0, 4.0) * (0.6 / math.sqrt(S))
    row_index = jnp.arange(S)[:, None]
    col_index = jnp.arange(S)[None, :]
    strict = jnp.where(row_index > col_index, lower_part, 0.0)
    return strict + jnp.where(row_index == col_index, 1.0, 0.0) * diagonal[..., :, None]


def draw_block_count(key, part):
    key_first, key_second, key_full = jax.random.split(key, 3)
    layout = (LEVELS - 1, ROWS_SN * COLS_SN)
    multiplier = jax.random.randint(key_first, layout, 1, NB + 1)
    multiplicand = jax.random.randint(key_second, layout, 1, NB + 1)
    filled = (multiplier * multiplicand + NB - 1) // NB
    busiest = jax.random.randint(key_full, (LEVELS - 1, 1), 0, ROWS_SN * COLS_SN)
    filled = jnp.where(jnp.arange(ROWS_SN * COLS_SN)[None, :] == busiest, NB, filled)
    return filled.reshape(LEVELS - 1, ROWS_SN, COLS_SN).astype(jnp.int32)


def place_ends(array, key, smallest, largest):
    longest = array.shape.index(max(array.shape))
    spots = []
    for shift in (0, 1):
        where = [jax.random.randint(jax.random.fold_in(key, axis), (), 0, length) for axis, length in enumerate(array.shape)]
        where[longest] = (where[longest] + shift) % array.shape[longest]
        spots.append(tuple(where))
    return array.at[spots[0]].set(smallest).at[spots[1]].set(largest)


def shard_levels(key, shape, cuts, low, top_value):
    def one(axis_at, blocks):
        heights = jax.random.uniform(jax.random.fold_in(jax.random.fold_in(key, 6), axis_at), (blocks,), jnp.float32, low / len(cuts), top_value / len(cuts))
        return jnp.repeat(jnp.exp(heights), shape[axis_at] // blocks).reshape((-1,) + (1,) * (len(shape) - axis_at - 1))

    gain = one(*cuts[0])
    for cut in cuts[1:]:
        gain = gain * one(*cut)
    return gain


def noise(key, shape, spread, reach, shards=(), kind=jnp.bfloat16):
    drawn = spread * jax.random.normal(key, shape, jnp.float32)
    if shards:
        drawn = drawn * shard_levels(key, shape, shards, -0.22, 0.18)
    return jnp.clip(drawn, -reach, reach).astype(kind)


def setup_inputs(seed: int = 0) -> dict:
    streams_of = jax.random.split(jax.random.key(seed), 7)
    return {
        "rhs": noise(streams_of[0], (LEVELS, ROWS_SN, COLS_SN, S, NRHS), 1.0, 6.0, ((1, 4), (2, 8)), jnp.float32),
        "diag_inverse": draw_diag_inverse(jax.random.fold_in(streams_of[6], 71), 0),
        "update_blocks": noise(streams_of[2], (LEVELS - 1, ROWS_SN, COLS_SN, NB, S, S), (S * NB // 4) ** -0.5, 0.15625, ((1, 4), (2, 8)), jnp.float32),
        "source_slot": place_ends(jax.random.randint(streams_of[3], (LEVELS - 1, ROWS_SN, COLS_SN, NB), 0, ROWS_SN), jax.random.fold_in(streams_of[3], 1), 0, ROWS_SN - 1).astype(jnp.int32),
        "target_slot": place_ends(jax.random.randint(streams_of[4], (LEVELS - 1, ROWS_SN, COLS_SN, NB), 0, COLS_SN), jax.random.fold_in(streams_of[4], 1), 0, COLS_SN - 1).astype(jnp.int32),
        "block_count": draw_block_count(jax.random.fold_in(streams_of[6], 71), 0),
    }


def apply_inverse(inverse, values):
    return jnp.einsum("...st,...tn->...sn", inverse, values, precision=lax.Precision.HIGHEST)


def apply_transposed(inverse, values):
    return jnp.einsum("...ts,...tn->...sn", inverse, values, precision=lax.Precision.HIGHEST)


def reference(rhs, diag_inverse, update_blocks, source_slot, target_slot, block_count):
    precise = lax.Precision.HIGHEST
    levels, row_count, col_count, block_width, right_count = rhs.shape
    slot_count = update_blocks.shape[3]
    columns = jnp.arange(col_count, dtype=jnp.int32)[:, None]
    forward = [apply_inverse(diag_inverse[0], rhs[0])]
    for level_index in range(1, levels):
        previous = forward[-1]

        def row_terms(inputs, previous=previous):
            tile_stack, sources, targets, filled = inputs
            active = (jnp.arange(slot_count, dtype=jnp.int32)[None, :] < filled[:, None]).astype(jnp.float32)
            chosen = previous[sources, columns]
            products = jnp.einsum("cbst,cbtn->cbsn", tile_stack, chosen, precision=precise) * active[:, :, None, None]
            base_terms = jnp.zeros((col_count, block_width, right_count), jnp.float32)
            return base_terms.at[targets.reshape(-1)].add(products.reshape(-1, block_width, right_count))

        updates = lax.map(row_terms, (update_blocks[level_index - 1], source_slot[level_index - 1],
                                      target_slot[level_index - 1], block_count[level_index - 1]))
        forward.append(apply_inverse(diag_inverse[level_index], rhs[level_index] - updates))
    backward = [apply_transposed(diag_inverse[levels - 1], forward[levels - 1])]
    for level_index in range(levels - 2, -1, -1):
        following = backward[0]

        def row_back(totals, inputs):
            tile_stack, sources, targets, filled, solved_row = inputs
            active = (jnp.arange(slot_count, dtype=jnp.int32)[None, :] < filled[:, None]).astype(jnp.float32)
            chosen = solved_row[targets]
            products = jnp.einsum("cbts,cbtn->cbsn", tile_stack, chosen, precision=precise) * active[:, :, None, None]
            return totals.at[sources, columns].add(products), None

        start_totals = jnp.zeros((row_count, col_count, block_width, right_count), jnp.float32)
        totals, unused = lax.scan(row_back, start_totals,
                                  (update_blocks[level_index], source_slot[level_index], target_slot[level_index],
                                   block_count[level_index], following))
        backward.insert(0, apply_transposed(diag_inverse[level_index], forward[level_index] - totals))
    return jnp.stack(forward), jnp.stack(backward)
```

```python
import functools

import jax
import jax.numpy as jnp
from jax import lax
from jax.experimental import pallas as pl
from jax.experimental.pallas import tpu as pltpu
from jax.sharding import PartitionSpec as P

F32, BF16 = jnp.float32, jnp.bfloat16
MESH = pl.DeviceIdType.MESH
VMEM_BYTES = 60 * 1024 * 1024


def split(x):
    high = x.astype(BF16)
    return high, (x - high.astype(F32)).astype(BF16)


def dot(a, b):
    return jnp.dot(a, b, preferred_element_type=F32)


def merge_kernel(rows, cols, src, tgt, count, blocks, out, acc):
    level, part = pl.program_id(0), pl.program_id(1)
    width = blocks.shape[-1]
    acc[...] = jnp.zeros_like(acc)

    def add(b, _):
        t = tgt[level, b] - part * cols
        s = src[level, b]

        @pl.when((t >= 0) & (t < cols))
        def _():
            i = t * rows + s
            acc[i] += blocks[0, b]

        return 0

    lax.fori_loop(0, count[level], add, 0)

    def write(t, _):
        for s in range(rows):
            high, low = split(acc[t * rows + s])
            out[0, t, 0, :, s * width : (s + 1) * width] = high
            out[0, t, 1, :, s * width : (s + 1) * width] = low
        return 0

    lax.fori_loop(0, cols, write, 0)


def merge(blocks, src, tgt, count, rows, cols):
    steps, slots, width, _ = blocks.shape
    parts = max(1, rows * cols // 64)
    per = cols // parts
    return pl.pallas_call(
        functools.partial(merge_kernel, rows, per),
        grid=(steps, parts),
        out_shape=jax.ShapeDtypeStruct((steps, cols, 2, width, rows * width), BF16),
        in_specs=[pl.BlockSpec(memory_space=pltpu.SMEM)] * 3
        + [pl.BlockSpec((1, slots, width, width), lambda l, p: (l, 0, 0, 0))],
        out_specs=pl.BlockSpec((1, per, 2, width, rows * width), lambda l, p: (l, p, 0, 0, 0)),
        scratch_shapes=[pltpu.VMEM((per * rows, width, width), F32)],
        compiler_params=pltpu.CompilerParams(vmem_limit_bytes=VMEM_BYTES),
    )(src, tgt, count, blocks)


def solve_kernel(
    rows, cols, halves, rhs, dinv, g_hbm, f_out, s_out,
    g, fg, psib, rsib, pown, rz, zg, q, rq, yt,
    g_sem, row_s, row_r, sib_s, sib_r, z_s, z_r,
    bz_s, bz_r, bsib_s, bsib_r, brow_s, brow_r,
):
    levels, _, _, S, total = rhs.shape
    n = total // halves
    steps = levels - 1
    chips = cols // 2
    kept = g.shape[0]
    me_r, me_c = lax.axis_index("row"), lax.axis_index("col")
    z, k = me_c // 2, me_c % 2
    sib = (me_r, 2 * z + 1 - k)
    unroll = rows * cols <= 32

    def row_dev(d):
        return (lax.rem(me_r + d, rows), me_c)

    def z_dev(d):
        return (me_r, 2 * lax.rem(z + d, chips) + k)

    barrier = pltpu.get_barrier_semaphore()
    peers = [row_dev(d) for d in range(1, rows)] + [z_dev(d) for d in range(1, chips)] + [sib]
    for dev in peers:
        pl.semaphore_signal(barrier, inc=1, device_id=dev, device_id_type=MESH)

    def g_copy(level):
        return pltpu.make_async_copy(g_hbm.at[level], g.at[level % kept], g_sem.at[level % kept])

    if kept == steps:
        for level in range(steps):
            g_copy(level).start()

    def g_ready(level, forward):
        if kept == steps:
            if forward:
                g_copy(level).wait()
        elif forward or level < steps - 1:
            g_copy(level).start()
            g_copy(level).wait()

    started = []

    def send(src, dst, s_sem, r_sem, dev):
        copy = pltpu.make_async_remote_copy(
            src_ref=src, dst_ref=dst, send_sem=s_sem, recv_sem=r_sem,
            device_id=dev, device_id_type=MESH,
        )
        copy.start()
        started.append(copy)

    def arrived(dst, s_sem, r_sem):
        pltpu.make_async_remote_copy(
            src_ref=dst, dst_ref=dst, send_sem=s_sem, recv_sem=r_sem,
            device_id=sib, device_id_type=MESH,
        ).wait_recv()

    def lanes(h):
        return slice(h * n, (h + 1) * n)

    def wide(x):
        return jnp.concatenate(split(x), axis=1)

    def left(a, w):
        p = dot(a, w)
        return (p[:S, :n] + p[:S, n:]) + (p[S:, :n] + p[S:, n:])

    def right(v, high, low):
        vh, vl = split(v)
        p = dot(jnp.concatenate([vh, vl], axis=0), high)
        return p[:n] + p[n:] + dot(vh, low)

    def forward_solve(level, h, v):
        d2 = jnp.concatenate(split(dinv[level, 0, 0]), axis=0)
        y = left(d2, wide(v))
        if level < steps:
            fg[level, h, me_r] = y
            if level == 0 and h == 0:
                pl.semaphore_wait(barrier, len(peers))
            for d in range(1, rows):
                ref = fg.at[level, h, me_r]
                send(ref, ref, row_s.at[level, h, d], row_r.at[level, h, d], row_dev(d))
        f_out[level, 0, 0, :, lanes(h)] = y
        yt[level, h] = y.T

    for h in range(halves):
        forward_solve(0, h, rhs[0, 0, 0, :, lanes(h)])

    for l in range(steps):
        g_ready(l, True)
        for h in range(halves):
            for d in range(1, rows):
                frm = lax.rem(me_r + rows - d, rows)
                arrived(fg.at[l, h, frm], row_s.at[l, h, d], row_r.at[l, h, d])
            w = wide(fg[l, h].reshape(rows * S, n))

            def term(t):
                return left(g[l % kept, t].reshape(2 * S, rows * S), w)

            def for_sib(c, _):
                psib[l, h, c] = term(2 * c + 1 - k)
                return 0

            def for_own(c, _):
                pown[l, h, c] = term(2 * c + k)
                return 0

            lax.fori_loop(0, chips, for_sib, 0, unroll=unroll)
            send(psib.at[l, h], rsib.at[l, h], sib_s.at[l, h], sib_r.at[l, h], sib)
            lax.fori_loop(0, chips, for_own, 0, unroll=unroll)
            arrived(rsib.at[l, h], sib_s.at[l, h], sib_r.at[l, h])
            for d in range(1, chips):
                c = lax.rem(z + d, chips)
                pown[l, h, c] += rsib[l, h, c]
                send(pown.at[l, h, c], rz.at[l, h, d], z_s.at[l, h, d], z_r.at[l, h, d], z_dev(d))
        for h in range(halves):
            u = pown[l, h, z] + rsib[l, h, z]
            for d in range(1, chips):
                arrived(rz.at[l, h, d], z_s.at[l, h, d], z_r.at[l, h, d])
                u += rz[l, h, d]
            forward_solve(l + 1, h, rhs[l + 1, 0, 0, :, lanes(h)] - u)

    def backward_solve(level, h, v):
        x = right(v, *split(dinv[level, 0, 0]))
        if level > 0:
            l = level - 1
            zg[l, h, me_c] = x
            ref = zg.at[l, h, me_c]
            for d in range(1, chips):
                send(ref, ref, bz_s.at[l, h, d], bz_r.at[l, h, d], z_dev(d))
            send(ref, ref, bsib_s.at[l, h, 0], bsib_r.at[l, h, 0], sib)
        s_out[level, 0, 0, :, lanes(h)] = x.T

    for h in range(halves):
        backward_solve(steps, h, yt[steps, h])

    for l in range(steps - 1, -1, -1):
        g_ready(l, False)
        for h in range(halves):
            def add(c, first):
                v = jnp.concatenate([zg[l, h, 2 * c], zg[l, h, 2 * c + 1]], axis=1)
                high = jnp.concatenate([g[l % kept, 2 * c, 0], g[l % kept, 2 * c + 1, 0]], axis=0)
                low = jnp.concatenate([g[l % kept, 2 * c, 1], g[l % kept, 2 * c + 1, 1]], axis=0)
                p = right(v, high, low)
                for s in range(rows):
                    part = p[:, s * S : (s + 1) * S]
                    q[l, h, s] = part if first else q[l, h, s] + part

            arrived(zg.at[l, h, 2 * z + 1 - k], bsib_s.at[l, h, 0], bsib_r.at[l, h, 0])
            add(z, True)
            for d in range(1, chips):
                c = lax.rem(z + chips - d, chips)
                ref = zg.at[l, h, 2 * c + k]
                arrived(ref, bz_s.at[l, h, d], bz_r.at[l, h, d])
                send(ref, ref, bsib_s.at[l, h, d], bsib_r.at[l, h, d], sib)
            for d in range(1, chips):
                c = lax.rem(z + chips - d, chips)
                arrived(zg.at[l, h, 2 * c + 1 - k], bsib_s.at[l, h, d], bsib_r.at[l, h, d])
                add(c, False)
            for d in range(1, rows):
                to = lax.rem(me_r + d, rows)
                send(q.at[l, h, to], rq.at[l, h, d], brow_s.at[l, h, d], brow_r.at[l, h, d], row_dev(d))
        for h in range(halves):
            u = q[l, h, me_r]
            for d in range(1, rows):
                arrived(rq.at[l, h, d], brow_s.at[l, h, d], brow_r.at[l, h, d])
                u += rq[l, h, d]
            backward_solve(l, h, yt[l, h] - u)

    for copy in started:
        copy.wait_send()


def solve(rhs, dinv, g, rows, cols):
    levels, _, _, S, total = rhs.shape
    halves = 2
    n = total // halves
    steps, chips = levels - 1, cols // 2
    kept = steps if rows * cols <= 64 else 1

    def vmem(*shape):
        return pltpu.VMEM(shape, F32)

    def sems(*shape):
        return [pltpu.SemaphoreType.DMA(shape)] * 2

    whole = pl.BlockSpec(memory_space=pltpu.VMEM)
    out = jax.ShapeDtypeStruct(rhs.shape, F32)
    return pl.pallas_call(
        functools.partial(solve_kernel, rows, cols, halves),
        out_shape=(out, out),
        in_specs=[whole, whole, pl.BlockSpec(memory_space=pl.ANY)],
        out_specs=(whole, whole),
        scratch_shapes=[
            pltpu.VMEM((kept,) + g.shape[1:], BF16),
            vmem(steps, halves, rows, S, n),
            vmem(steps, halves, chips, S, n),
            vmem(steps, halves, chips, S, n),
            vmem(steps, halves, chips, S, n),
            vmem(steps, halves, chips, S, n),
            vmem(steps, halves, cols, n, S),
            vmem(steps, halves, rows, n, S),
            vmem(steps, halves, rows, n, S),
            vmem(levels, halves, n, S),
            pltpu.SemaphoreType.DMA((kept,)),
            *sems(steps, halves, rows),
            *sems(steps, halves),
            *sems(steps, halves, chips),
            *sems(steps, halves, chips),
            *sems(steps, halves, chips),
            *sems(steps, halves, rows),
        ],
        compiler_params=pltpu.CompilerParams(
            collective_id=0, has_side_effects=True, vmem_limit_bytes=VMEM_BYTES
        ),
    )(rhs, dinv, g)


def solution(mesh):
    rows, cols = mesh.shape["row"], mesh.shape["col"]

    def per_device(rhs, diag_inverse, update_blocks, source_slot, target_slot, block_count):
        g = merge(
            update_blocks[:, 0, 0], source_slot[:, 0, 0], target_slot[:, 0, 0],
            block_count[:, 0, 0], rows, cols,
        )
        return solve(rhs, diag_inverse, g, rows, cols)

    in_specs = (
        P(None, "row", "col", None, None),
        P(None, "row", "col", None, None),
        P(None, "row", "col", None, None, None),
        P(None, "row", "col", None),
        P(None, "row", "col", None),
        P(None, "row", "col"),
    )
    out_specs = (P(None, "row", "col", None, None), P(None, "row", "col", None, None))
    return jax.shard_map(
        per_device, mesh=mesh, in_specs=in_specs, out_specs=out_specs, check_vma=False
    )
```

```python
import functools

import jax
import jax.numpy as jnp
from jax import lax
from jax.experimental import pallas as pl
from jax.experimental.pallas import tpu as pltpu
from jax.sharding import PartitionSpec as P

F32, BF16 = jnp.float32, jnp.bfloat16
MESH = pl.DeviceIdType.MESH
VMEM_BYTES = 60 * 1024 * 1024


def split(x):
    high = x.astype(BF16)
    return high, (x - high.astype(F32)).astype(BF16)


def dot(a, b):
    return jnp.dot(a, b, preferred_element_type=F32)


def merge_kernel(rows, cols, src, tgt, count, blocks, out, acc):
    level, part = pl.program_id(0), pl.program_id(1)
    width = blocks.shape[-1]
    acc[...] = jnp.zeros_like(acc)

    def add(b, _):
        t = tgt[level, 0, 0, b] - part * cols
        s = src[level, 0, 0, b]

        @pl.when((t >= 0) & (t < cols))
        def _():
            i = t * rows + s
            acc[i] += blocks[b]

        return 0

    lax.fori_loop(0, count[level, 0, 0], add, 0)

    def write(t, _):
        for s in range(rows):
            high, low = split(acc[t * rows + s])
            out[0, t, 0, :, s * width : (s + 1) * width] = high
            out[0, t, 1, :, s * width : (s + 1) * width] = low
        return 0

    lax.fori_loop(0, cols, write, 0)


def merge(blocks, src, tgt, count, rows, cols):
    steps, _, _, slots, width, _ = blocks.shape
    parts = max(1, rows * cols // 64)
    per = cols // parts
    return pl.pallas_call(
        functools.partial(merge_kernel, rows, per),
        grid=(steps, parts),
        out_shape=jax.ShapeDtypeStruct((steps, cols, 2, width, rows * width), BF16),
        in_specs=[pl.BlockSpec(memory_space=pltpu.SMEM)] * 3
        + [pl.BlockSpec((None, None, None, slots, width, width), lambda l, p: (l, 0, 0, 0, 0, 0))],
        out_specs=pl.BlockSpec((1, per, 2, width, rows * width), lambda l, p: (l, p, 0, 0, 0)),
        scratch_shapes=[pltpu.VMEM((per * rows, width, width), F32)],
        compiler_params=pltpu.CompilerParams(vmem_limit_bytes=VMEM_BYTES),
    )(src, tgt, count, blocks)


def solve_kernel(
    rows, cols, halves, rhs, dinv, g_hbm, f_out, s_out,
    g, fg, psib, rsib, pown, rz, zg, q, rq, yt,
    g_sem, row_s, row_r, sib_s, sib_r, z_s, z_r,
    bz_s, bz_r, bsib_s, bsib_r, brow_s, brow_r,
):
    levels, _, _, S, total = rhs.shape
    n = total // halves
    steps = levels - 1
    chips = cols // 2
    kept = g.shape[0]
    me_r, me_c = lax.axis_index("row"), lax.axis_index("col")
    z, k = me_c // 2, me_c % 2
    sib = (me_r, 2 * z + 1 - k)
    unroll = rows * cols <= 32

    def row_dev(d):
        return (lax.rem(me_r + d, rows), me_c)

    def z_dev(d):
        return (me_r, 2 * lax.rem(z + d, chips) + k)

    barrier = pltpu.get_barrier_semaphore()
    peers = [row_dev(d) for d in range(1, rows)] + [z_dev(d) for d in range(1, chips)] + [sib]
    for dev in peers:
        pl.semaphore_signal(barrier, inc=1, device_id=dev, device_id_type=MESH)

    def g_copy(level):
        return pltpu.make_async_copy(g_hbm.at[level], g.at[level % kept], g_sem.at[level % kept])

    if kept == steps:
        for level in range(steps):
            g_copy(level).start()

    def g_ready(level, forward):
        if kept == steps:
            if forward:
                g_copy(level).wait()
        elif forward or level < steps - 1:
            g_copy(level).start()
            g_copy(level).wait()

    started = []

    def send(src, dst, s_sem, r_sem, dev):
        copy = pltpu.make_async_remote_copy(
            src_ref=src, dst_ref=dst, send_sem=s_sem, recv_sem=r_sem,
            device_id=dev, device_id_type=MESH,
        )
        copy.start()
        started.append(copy)

    def arrived(dst, s_sem, r_sem):
        pltpu.make_async_remote_copy(
            src_ref=dst, dst_ref=dst, send_sem=s_sem, recv_sem=r_sem,
            device_id=sib, device_id_type=MESH,
        ).wait_recv()

    def lanes(h):
        return slice(h * n, (h + 1) * n)

    def wide(x):
        return jnp.concatenate(split(x), axis=1)

    def left(a, w):
        p = dot(a, w)
        return (p[:S, :n] + p[:S, n:]) + (p[S:, :n] + p[S:, n:])

    def right(v, high, low):
        vh, vl = split(v)
        p = dot(jnp.concatenate([vh, vl], axis=0), high)
        return p[:n] + p[n:] + dot(vh, low)

    def forward_solve(level, h, v):
        d2 = jnp.concatenate(split(dinv[level, 0, 0]), axis=0)
        y = left(d2, wide(v))
        if level < steps:
            fg[level, h, me_r] = y
            if level == 0 and h == 0:
                pl.semaphore_wait(barrier, len(peers))
            for d in range(1, rows):
                ref = fg.at[level, h, me_r]
                send(ref, ref, row_s.at[level, h, d], row_r.at[level, h, d], row_dev(d))
        f_out[level, 0, 0, :, lanes(h)] = y
        yt[level, h] = y.T

    def forward_products(l, h):
        for d in range(1, rows):
            frm = lax.rem(me_r + rows - d, rows)
            arrived(fg.at[l, h, frm], row_s.at[l, h, d], row_r.at[l, h, d])
        w = wide(fg[l, h].reshape(rows * S, n))

        def term(t):
            return left(g[l % kept, t].reshape(2 * S, rows * S), w)

        def for_sib(c, _):
            psib[l, h, c] = term(2 * c + 1 - k)
            return 0

        def for_own(c, _):
            pown[l, h, c] = term(2 * c + k)
            return 0

        lax.fori_loop(0, chips, for_sib, 0, unroll=unroll)
        send(psib.at[l, h], rsib.at[l, h], sib_s.at[l, h], sib_r.at[l, h], sib)
        lax.fori_loop(0, chips, for_own, 0, unroll=unroll)
        arrived(rsib.at[l, h], sib_s.at[l, h], sib_r.at[l, h])
        for d in range(1, chips):
            c = lax.rem(z + d, chips)
            pown[l, h, c] += rsib[l, h, c]
            send(pown.at[l, h, c], rz.at[l, h, d], z_s.at[l, h, d], z_r.at[l, h, d], z_dev(d))

    def forward_next(l, h):
        u = pown[l, h, z] + rsib[l, h, z]
        for d in range(1, chips):
            arrived(rz.at[l, h, d], z_s.at[l, h, d], z_r.at[l, h, d])
            u += rz[l, h, d]
        forward_solve(l + 1, h, rhs[l + 1, 0, 0, :, lanes(h)] - u)

    def backward_solve(level, h, v):
        x = right(v, *split(dinv[level, 0, 0]))
        if level > 0:
            l = level - 1
            zg[l, h, me_c] = x
            ref = zg.at[l, h, me_c]
            for d in range(1, chips):
                send(ref, ref, bz_s.at[l, h, d], bz_r.at[l, h, d], z_dev(d))
            send(ref, ref, bsib_s.at[l, h, 0], bsib_r.at[l, h, 0], sib)
        s_out[level, 0, 0, :, lanes(h)] = x.T

    def backward_products(l, h):
        def add(c, first):
            v = jnp.concatenate([zg[l, h, 2 * c], zg[l, h, 2 * c + 1]], axis=1)
            high = jnp.concatenate([g[l % kept, 2 * c, 0], g[l % kept, 2 * c + 1, 0]], axis=0)
            low = jnp.concatenate([g[l % kept, 2 * c, 1], g[l % kept, 2 * c + 1, 1]], axis=0)
            p = right(v, high, low)
            for s in range(rows):
                part = p[:, s * S : (s + 1) * S]
                q[l, h, s] = part if first else q[l, h, s] + part

        arrived(zg.at[l, h, 2 * z + 1 - k], bsib_s.at[l, h, 0], bsib_r.at[l, h, 0])
        add(z, True)
        for d in range(1, chips):
            c = lax.rem(z + chips - d, chips)
            ref = zg.at[l, h, 2 * c + k]
            arrived(ref, bz_s.at[l, h, d], bz_r.at[l, h, d])
            send(ref, ref, bsib_s.at[l, h, d], bsib_r.at[l, h, d], sib)
        for d in range(1, chips):
            c = lax.rem(z + chips - d, chips)
            arrived(zg.at[l, h, 2 * c + 1 - k], bsib_s.at[l, h, d], bsib_r.at[l, h, d])
            add(c, False)
        for d in range(1, rows):
            to = lax.rem(me_r + d, rows)
            send(q.at[l, h, to], rq.at[l, h, d], brow_s.at[l, h, d], brow_r.at[l, h, d], row_dev(d))

    def backward_next(l, h):
        u = q[l, h, me_r]
        for d in range(1, rows):
            arrived(rq.at[l, h, d], brow_s.at[l, h, d], brow_r.at[l, h, d])
            u += rq[l, h, d]
        backward_solve(l, h, yt[l, h] - u)

    for h in range(halves):
        forward_solve(0, h, rhs[0, 0, 0, :, lanes(h)])
    g_ready(0, True)
    for h in range(halves):
        forward_products(0, h)
    for l in range(steps):
        if l + 1 < steps:
            g_ready(l + 1, True)
        for h in range(halves):
            forward_next(l, h)
            if l + 1 < steps:
                forward_products(l + 1, h)
            else:
                backward_solve(steps, h, yt[steps, h])
    for l in range(steps - 1, -1, -1):
        g_ready(l, False)
        for h in range(halves):
            backward_products(l, h)
        for h in range(halves):
            backward_next(l, h)

    for copy in started:
        copy.wait_send()


def solve(rhs, dinv, g, rows, cols):
    levels, _, _, S, total = rhs.shape
    halves = 2
    n = total // halves
    steps, chips = levels - 1, cols // 2
    kept = steps if rows * cols <= 64 else 1

    def vmem(*shape):
        return pltpu.VMEM(shape, F32)

    def sems(*shape):
        return [pltpu.SemaphoreType.DMA(shape)] * 2

    whole = pl.BlockSpec(memory_space=pltpu.VMEM)
    out = jax.ShapeDtypeStruct(rhs.shape, F32)
    return pl.pallas_call(
        functools.partial(solve_kernel, rows, cols, halves),
        out_shape=(out, out),
        in_specs=[whole, whole, pl.BlockSpec(memory_space=pl.ANY)],
        out_specs=(whole, whole),
        scratch_shapes=[
            pltpu.VMEM((kept,) + g.shape[1:], BF16),
            vmem(steps, halves, rows, S, n),
            vmem(steps, halves, chips, S, n),
            vmem(steps, halves, chips, S, n),
            vmem(steps, halves, chips, S, n),
            vmem(steps, halves, chips, S, n),
            vmem(steps, halves, cols, n, S),
            vmem(steps, halves, rows, n, S),
            vmem(steps, halves, rows, n, S),
            vmem(levels, halves, n, S),
            pltpu.SemaphoreType.DMA((kept,)),
            *sems(steps, halves, rows),
            *sems(steps, halves),
            *sems(steps, halves, chips),
            *sems(steps, halves, chips),
            *sems(steps, halves, chips),
            *sems(steps, halves, rows),
        ],
        compiler_params=pltpu.CompilerParams(
            collective_id=0, has_side_effects=True, vmem_limit_bytes=VMEM_BYTES
        ),
    )(rhs, dinv, g)


def place_kernel(f_in, s_in, f_out, s_out):
    f_out[...] = f_in[...]
    s_out[...] = s_in[...]


def place(f, s):
    block = pl.BlockSpec((2,) + f.shape[1:], lambda l: (l, 0, 0, 0, 0))
    out = jax.ShapeDtypeStruct(f.shape, F32)
    return pl.pallas_call(
        place_kernel, grid=(f.shape[0] // 2,), out_shape=(out, out),
        in_specs=[block, block], out_specs=(block, block),
    )(f, s)


def solution(mesh):
    rows, cols = mesh.shape["row"], mesh.shape["col"]

    def per_device(rhs, diag_inverse, update_blocks, source_slot, target_slot, block_count):
        g = merge(
            update_blocks, source_slot, target_slot, block_count, rows, cols,
        )
        return place(*solve(rhs, diag_inverse, g, rows, cols))

    in_specs = (
        P(None, "row", "col", None, None),
        P(None, "row", "col", None, None),
        P(None, "row", "col", None, None, None),
        P(None, "row", "col", None),
        P(None, "row", "col", None),
        P(None, "row", "col"),
    )
    out_specs = (P(None, "row", "col", None, None), P(None, "row", "col", None, None))
    return jax.shard_map(
        per_device, mesh=mesh, in_specs=in_specs, out_specs=out_specs, check_vma=False
    )
```
